32 devices in a mesh: dp: 2 (over core), ctx: 16 (over z, y, x).
Axes of the slice: x: 2, y: 2, z: 4, core: 2. Of those that a mesh axis runs over, the one named last changes fastest.
Arguments:
- queries: bfloat16 [2, 2048, 2048], P('dp', 'ctx'), may hold values from -6 to 6
- keys: bfloat16 [2, 2048, 2048], P('dp', 'ctx'), may hold values from -6 to 6
- values: bfloat16 [2, 2048, 2048], P('dp', 'ctx'), may hold values from -6 to 6
- doc_ids: int32 [2, 32], P('dp', 'ctx'), may hold values from 0 to 7, never falling along the last dimension, each value on 1 to 8 neighbouring positions
- feat_weight: bfloat16 [128, 160], replicated, may hold values from -0.5 to 0.5
- out_grad: bfloat16 [2, 2048, 2048], P('dp', 'ctx'), may hold values from -6 to 6
Outputs:
- out: float32 [2, 2048, 2048], P('dp', 'ctx')
- query_grad: float32 [2, 2048, 2048], P('dp', 'ctx')
- key_grad: float32 [2, 2048, 2048], P('dp', 'ctx')
- value_grad: float32 [2, 2048, 2048], P('dp', 'ctx')
- new_weight: float32 [128, 160], replicated
The draws below stay inside these ranges and needn't reach their ends.
Inputs may be any that keep to these rules, and one draw needn't show every extreme that they name: `doc_ids`: along each sequence the ids never fall; every id names one run of 1 to 8 blocks, and one run has exactly 8 blocks.
All inputs are finite; a program needn't handle non-finite values.
Results may differ from the reference program's by a relative error of at most 0.015.
Values sent between devices are 32-bit elements; how exact they have to be, the bound alone decides.
A program may use at most 64 MiB of HBM per device.

```python
import math
import jax
import jax.numpy as jnp
import numpy as np
from jax import lax

H = 16
DH = 128
F = 160
BLOCK = 64
DOCS = 8
T_DEV = 128
SEQS = 2
LEN = 2048
BLOCKS = 32
MOST = 8
N_CTX = 16


def shard_levels(own_key, extent, pieces, smallest, largest):
    def one(dim, shards_of):
        draws = jax.random.uniform(jax.random.fold_in(jax.random.fold_in(own_key, 6), dim), (shards_of,), jnp.float32, smallest / len(pieces), largest / len(pieces))
        return jnp.repeat(jnp.exp(draws), extent[dim] // shards_of).reshape((-1,) + (1,) * (len(extent) - dim - 1))

    factor_of = one(*pieces[0])
    for cut in pieces[1:]:
        factor_of = factor_of * one(*cut)
    return factor_of


def split_up(number_of, total, most, skew):
    portions = [(1 << 20) // math.isqrt(standing ** skew) + 1 for standing in range(2, number_of + 1)]
    surplus, counts = total - most - (number_of - 1), [1] * (number_of - 1)
    while surplus > 0:
        candidates = [i for i in range(number_of - 1) if counts[i] < most]
        whole, budget = sum([portions[i] for i in candidates]), surplus
        for i in candidates:
            extra = min(most - counts[i], max(1, budget * portions[i] // whole), surplus)
            counts[i] = counts[i] + extra
            surplus = surplus - extra
    return np.array([most] + counts)


def uneven_parts(stream_key, count, total, reach, slope):
    if count == 2:
        one = jax.random.randint(stream_key, (), max(1, total - reach), min(reach, total - 1) + 1)
        return jnp.stack([one, total - one])
    tallies = jnp.asarray(split_up(count, total, reach, slope), jnp.int32)
    pairs = (count - 1) // 2
    donor, receiver = tallies[1:1 + 2 * pairs:2], tallies[2:2 + 2 * pairs:2]
    slack = jnp.minimum(donor - 1, reach - receiver)
    moved = jax.random.randint(jax.random.fold_in(stream_key, 1), (pairs,), 0, 1 << 20) % (slack + 1)
    tallies = tallies.at[1:1 + 2 * pairs:2].set(donor - moved).at[2:2 + 2 * pairs:2].set(receiver + moved)
    return tallies[jax.random.permutation(jax.random.fold_in(stream_key, 2), count)]


def centred(rng, dims, spread, limit, cuts=(), dtype=jnp.bfloat16):
    drawn = spread * jax.random.normal(rng, dims, jnp.float32)
    if cuts:
        drawn = drawn * shard_levels(rng, dims, cuts, -0.22, 0.18)
    return jnp.clip(drawn, -limit, limit).astype(dtype)


def setup_inputs(seed: int = 0) -> dict:
    splits = jax.random.split(jax.random.key(seed), 7)
    return {
        "queries": centred(splits[0], (SEQS, LEN, H * DH), 1.0, 6.0, ((0, 2), (1, 16))),
        "keys": centred(splits[1], (SEQS, LEN, H * DH), 1.0, 6.0, ((0, 2), (1, 16))),
        "values": centred(splits[2], (SEQS, LEN, H * DH), 1.0, 6.0, ((0, 2), (1, 16))),
        "doc_ids": jax.vmap(lambda own: jnp.searchsorted(jnp.cumsum(uneven_parts(own, DOCS, BLOCKS, MOST, 0)), jnp.arange(BLOCKS), side="right"))(jax.random.split(splits[3], SEQS)).reshape((SEQS, BLOCKS)).astype(jnp.int32),
        "feat_weight": centred(splits[4], (DH, F), DH ** -0.5, 0.5),
        "out_grad": centred(splits[5], (SEQS, LEN, H * DH), 1.0, 6.0, ((0, 2), (1, 16))),
    }


HIGH = lax.Precision.HIGHEST
RATE = 0.5
EPSILON = 1e-06

def features(proj):
    return (1.0 + proj + 0.5 * proj * proj).astype(jnp.bfloat16)

def section_local(query3, key3, docs, weight):
    weight_f = weight.astype(jnp.float32)
    proj_q = jnp.einsum('thd,df->thf', query3.astype(jnp.float32), weight_f, precision=HIGH)
    proj_k = jnp.einsum('thd,df->thf', key3.astype(jnp.float32), weight_f, precision=HIGH)
    feat_q = features(proj_q)
    feat_k = features(proj_k)
    order = jnp.arange(docs.shape[0])
    mask = jnp.logical_and(order[None, :] <= order[:, None], docs[None, :] == docs[:, None]).astype(jnp.float32)
    raw = jnp.einsum('thf,shf->hts', feat_q.astype(jnp.float32), feat_k.astype(jnp.float32), precision=HIGH)
    probs = (raw * mask[None]).astype(jnp.bfloat16)
    return (proj_q, proj_k, feat_q, feat_k, mask, probs)

def section_forward(query3, key3, value3, docs, weight, state_in, norm_in, pre_end):
    proj_q, proj_k, feat_q, feat_k, mask, probs = section_local(query3, key3, docs, weight)
    feat_qf = feat_q.astype(jnp.float32)
    value_f = value3.astype(jnp.float32)
    in_mask = (docs == pre_end).astype(jnp.float32)
    probs_f = probs.astype(jnp.float32)
    num_local = jnp.einsum('hts,shd->thd', probs_f, value_f, precision=HIGH)
    den_local = lax.optimization_barrier(jnp.sum(probs_f, axis=2)).T
    den = den_local + jnp.einsum('thf,hf->th', feat_qf, norm_in, precision=HIGH) * in_mask[:, None]
    out = (num_local + jnp.einsum('thf,hfd->thd', feat_qf, state_in, precision=HIGH) * in_mask[:, None, None]) / den[:, :, None]
    return (proj_q, proj_k, feat_q, feat_k, mask, probs, in_mask, den, out)

def one_sequence(queries, keys, values, doc_ids, weight, out_grad):
    query4 = queries.reshape(N_CTX, T_DEV, H, DH)
    key4 = keys.reshape(N_CTX, T_DEV, H, DH)
    value4 = values.reshape(N_CTX, T_DEV, H, DH)
    grad4 = out_grad.reshape(N_CTX, T_DEV, H, DH)
    docs4 = jnp.repeat(doc_ids, BLOCK).astype(jnp.int32).reshape(N_CTX, T_DEV)

    def forward_step(carry, items):
        state, norm, end = carry
        query3, key3, value3, docs = items
        proj_q, proj_k, feat_q, feat_k, mask, probs = section_local(query3, key3, docs, weight)
        tail_mask = (docs == docs[-1]).astype(jnp.float32)
        feat_kf = feat_k.astype(jnp.float32)
        tail_state = jnp.einsum('thf,thd->hfd', feat_kf * tail_mask[:, None, None], value3.astype(jnp.float32), precision=HIGH)
        tail_norm = jnp.einsum('thf,t->hf', feat_kf, tail_mask, precision=HIGH)
        joined = docs[-1] == end
        new_state = tail_state + jnp.where(joined, state, jnp.zeros_like(state))
        new_norm = tail_norm + jnp.where(joined, norm, jnp.zeros_like(norm))
        return ((new_state, new_norm, docs[-1].astype(jnp.int32)), (state, norm, end))
    start = (jnp.zeros((H, F, DH), jnp.float32), jnp.zeros((H, F), jnp.float32), jnp.array(-1, jnp.int32))
    _, (states, norms, ends) = lax.scan(forward_step, start, (query4, key4, value4, docs4))

    def backward_step(carry, items):
        adjoint, adjoint_norm, key_doc, grad_total = carry
        query3, key3, value3, grad3, docs, state_in, norm_in, pre_end = items
        proj_q, proj_k, feat_q, feat_k, mask, probs, in_mask, den, out = section_forward(query3, key3, value3, docs, weight, state_in, norm_in, pre_end)
        feat_qf = feat_q.astype(jnp.float32)
        feat_kf = feat_k.astype(jnp.float32)
        value_f = value3.astype(jnp.float32)
        grad_f = grad3.astype(jnp.float32)
        scaled = grad_f / den[:, :, None]
        scaled_b = scaled.astype(jnp.bfloat16).astype(jnp.float32)
        drift = -lax.optimization_barrier(jnp.sum(grad_f * out, axis=2)) / den
        dscore = jnp.einsum('thd,shd->hts', scaled_b, value_f, precision=HIGH) + drift.T[:, :, None]
        dprobs = (dscore * mask[None]).astype(jnp.bfloat16).astype(jnp.float32)
        out_mask = (docs == key_doc).astype(jnp.float32)
        grad_fq = jnp.einsum('hts,shf->thf', dprobs, feat_kf, precision=HIGH) + (jnp.einsum('hfd,thd->thf', state_in, scaled, precision=HIGH) + norm_in[None] * drift[:, :, None]) * in_mask[:, None, None]
        grad_fk = jnp.einsum('hts,thf->shf', dprobs, feat_qf, precision=HIGH) + (jnp.einsum('hfd,shd->shf', adjoint, value_f, precision=HIGH) + adjoint_norm[None]) * out_mask[:, None, None]
        value_grad = jnp.einsum('hts,thd->shd', probs.astype(jnp.float32), scaled_b, precision=HIGH) + jnp.einsum('shf,hfd->shd', feat_kf, adjoint, precision=HIGH) * out_mask[:, None, None]
        grad_pq = (grad_fq * (1.0 + proj_q)).astype(jnp.bfloat16).astype(jnp.float32)
        grad_pk = (grad_fk * (1.0 + proj_k)).astype(jnp.bfloat16).astype(jnp.float32)
        weight_f = weight.astype(jnp.float32)
        query_grad = jnp.einsum('thf,df->thd', grad_pq, weight_f, precision=HIGH)
        key_grad = jnp.einsum('thf,df->thd', grad_pk, weight_f, precision=HIGH)
        grad_here = jnp.einsum('thd,thf->df', query3.astype(jnp.float32), grad_pq, precision=HIGH) + jnp.einsum('thd,thf->df', key3.astype(jnp.float32), grad_pk, precision=HIGH)
        head_mask = (docs == docs[0]).astype(jnp.float32)
        head_state = jnp.einsum('thf,thd->hfd', feat_qf * head_mask[:, None, None], scaled, precision=HIGH)
        head_norm = jnp.einsum('thf,th->hf', feat_qf * head_mask[:, None, None], drift, precision=HIGH)
        joined = docs[0] == key_doc
        new_adjoint = head_state + jnp.where(joined, adjoint, jnp.zeros_like(adjoint))
        new_norm = head_norm + jnp.where(joined, adjoint_norm, jnp.zeros_like(adjoint_norm))
        carry = (new_adjoint, new_norm, docs[0].astype(jnp.int32), grad_total + grad_here)
        return (carry, (out, query_grad, key_grad, value_grad))
    start = (jnp.zeros((H, F, DH), jnp.float32), jnp.zeros((H, F), jnp.float32), jnp.array(-1, jnp.int32), jnp.zeros((DH, F), jnp.float32))
    final, results = lax.scan(backward_step, start, (query4, key4, value4, grad4, docs4, states, norms, ends), reverse=True)
    shaped = tuple((item.reshape(LEN, H * DH) for item in results))
    return (shaped, final[3])

def reference(queries, keys, values, doc_ids, feat_weight, out_grad):
    outs = []
    weight_grad = jnp.zeros((DH, F), jnp.float32)
    for index in range(SEQS):
        shaped, grad_part = one_sequence(queries[index], keys[index], values[index], doc_ids[index], feat_weight, out_grad[index])
        outs.append(shaped)
        weight_grad = weight_grad + grad_part
    stacked = tuple((jnp.stack([item[position] for item in outs]) for position in range(4)))
    scale = lax.rsqrt(jnp.mean(weight_grad * weight_grad) + EPSILON)
    new_weight = feat_weight.astype(jnp.float32) - RATE * weight_grad * scale
    return (stacked[0], stacked[1], stacked[2], stacked[3], new_weight)
```

```python
import functools

import jax
import jax.numpy as jnp
from jax import lax
from jax.experimental import pallas as pl
from jax.experimental.pallas import tpu as pltpu
from jax.sharding import PartitionSpec as P

H = 16
DH = 128
F = 160
BLOCK = 64
RATE = 0.5
EPSILON = 1e-06
STEP = 4
CHUNK = 4
MESH = pl.DeviceIdType.MESH
BF = jnp.bfloat16
F32 = jnp.float32
LIMIT = 56 * 1024 * 1024


def dot(a, b, dims):
    return lax.dot_general(a, b, ((dims[:1], dims[1:]), ((), ())), preferred_element_type=F32)


def features(proj):
    return (1.0 + proj + 0.5 * proj * proj).astype(BF)


def halves(x):
    high = x.astype(BF)
    return high, (x - high.astype(F32)).astype(BF)


def row_docs(doc_ref, shape, dim):
    place = lax.broadcasted_iota(jnp.int32, shape, dim) // BLOCK
    docs = jnp.zeros(shape, F32)
    for block in range(doc_ref.shape[1]):
        docs = jnp.where(place == block, doc_ref[0, block].astype(F32), docs)
    return docs


def same(a, b):
    return jnp.where(a == b, 1.0, 0.0)


def head_columns(head):
    return pl.ds(pl.multiple_of(head * DH, DH), DH)


def local_kernel(doc_ref, q_ref, k_ref, v_ref, w_ref, fq_ref, probs_ref, state_ref, norm_ref, den_ref):
    tokens = q_ref.shape[0]
    rows = row_docs(doc_ref, (tokens, 1), 0)
    mask = jnp.logical_and(
        lax.broadcasted_iota(jnp.int32, (tokens, tokens), 1)
        <= lax.broadcasted_iota(jnp.int32, (tokens, tokens), 0),
        rows == row_docs(doc_ref, (1, tokens), 1),
    )
    tail = same(rows, doc_ref[0, doc_ref.shape[1] - 1].astype(F32))
    weight = w_ref[...]
    ones = jnp.ones((tokens, DH), BF)
    norms = []
    for j in range(STEP):
        part = slice(j * DH, (j + 1) * DH)
        value = v_ref[:, part]
        feat_q = features(dot(q_ref[:, part], weight, (1, 0)))
        feat_k = features(dot(k_ref[:, part], weight, (1, 0)))
        probs = jnp.where(mask, dot(feat_q, feat_k, (1, 1)), 0.0).astype(BF)
        tail_k = feat_k.astype(F32) * tail
        fq_ref[j] = feat_q
        probs_ref[j] = probs
        den_ref[:, part] = dot(probs, ones, (1, 0))
        state_ref[j] = dot(tail_k.astype(BF), value, (0, 0))
        norms.append(jnp.sum(tail_k, axis=0, keepdims=True))
    for j in range(STEP):
        norm_ref[j] = jnp.concatenate([norms[j], jnp.zeros((1, 256 - F), F32)], axis=1)


def bits(count):
    return [1 << r for r in range(count.bit_length() - 1)]


def exchange_kernel(
    n, group, doc_ref, fq_ref, state_ref, norm_ref, den0_ref, g_ref,
    s_ref, a_ref, nin_ref, den_ref, edge_ref,
    msg, note, table, got_msg, got_note, adj, part, suffix, got,
    ms, mr, ns, nr, send, recv,
):
    me = lax.axis_index("ctx")
    rounds = bits(group)
    last_round = len(rounds)
    chunks = H // CHUNK

    barrier = pltpu.get_barrier_semaphore()
    for k in range(1, group + 1):
        for target in (lax.rem(me + k, n), lax.rem(me + n - k, n)):
            pl.semaphore_signal(barrier, inc=1, device_id={"ctx": target}, device_id_type=MESH)

    last = doc_ref[0, doc_ref.shape[1] - 1].astype(F32)
    first = doc_ref[0, 0].astype(F32)
    which = lax.broadcasted_iota(jnp.int32, (8, 256), 0)
    tile = jnp.where(which == 0, last, jnp.where(which == 1, first, 0.0))
    note[...] = tile
    table[group] = tile
    for h in range(H):
        msg[h : h + 1, :] = norm_ref[h]
    msg[H : H + 8, :] = tile
    pl.semaphore_wait(barrier, 2 * group)

    small = []
    for k in range(1, group + 1):
        small.append(pltpu.make_async_remote_copy(
            src_ref=msg, dst_ref=got_msg.at[k - 1], send_sem=ms.at[k - 1], recv_sem=mr.at[k - 1],
            device_id={"ctx": lax.rem(me + k, n)}, device_id_type=MESH))
        small.append(pltpu.make_async_remote_copy(
            src_ref=note, dst_ref=got_note.at[k - 1], send_sem=ns.at[k - 1], recv_sem=nr.at[k - 1],
            device_id={"ctx": lax.rem(me + n - k, n)}, device_id_type=MESH))
    for copy in small:
        copy.start()

    def copy_of(kind, c, r):
        heads = pl.ds(c * CHUNK, CHUNK)
        if r < last_round:
            b = rounds[r]
            target = me + b - 2 * b * lax.rem(me // b, 2)
        else:
            target = me + group if kind == 0 else me - group
        if r == 0 and last_round > 0:
            source = (state_ref if kind == 0 else adj).at[heads]
        elif r < last_round:
            source = part.at[kind, r - 1, heads]
        else:
            source = suffix.at[kind, heads]
        slot = (kind * chunks + c) * (last_round + 1) + r
        return pltpu.make_async_remote_copy(
            src_ref=source, dst_ref=got.at[kind, r, heads], send_sem=send.at[slot], recv_sem=recv.at[slot],
            device_id={"ctx": target}, device_id_type=MESH)

    can_up = me + group < n
    can_down = me >= group

    def start(kind, c, r):
        if r < last_round:
            copy_of(kind, c, r).start()
        else:
            @pl.when(can_up if kind == 0 else can_down)
            def _():
                copy_of(kind, c, r).start()

    for c in range(chunks):
        start(0, c, 0)

    for k in range(group):
        small[2 * k].wait_recv()
        small[2 * k + 1].wait_recv()
    for k in range(1, group + 1):
        table[group - k] = got_msg[k - 1, H : H + 8, :]
        table[group + k] = got_note[k - 1]

    def doc_at(index, kind):
        return table[index - me + group][kind : kind + 1, :]

    before = table[group - 1][0:1, :]
    after = table[group + 1][1:2, :]
    edge_ref[0:1, :] = before[:, :DH]
    edge_ref[1:2, :] = after[:, :DH]
    edge_ref[2:8, :] = jnp.zeros((6, DH), F32)
    norm = jnp.zeros((H, 256), F32)
    for k in range(1, group + 1):
        w = same(got_msg[k - 1, H : H + 1, :], before) * jnp.where(me >= k, 1.0, 0.0)
        norm = norm + w * got_msg[k - 1, 0:H, :]
    for h in range(H):
        nin_ref[h] = norm[h : h + 1, :]

    tokens = g_ref.shape[0]
    rows = row_docs(doc_ref, (tokens, 1), 0)
    inside = same(rows, before[:, :DH])
    head = same(rows, first)

    def adjoint_of(h, carry):
        columns = head_columns(h)
        feat = fq_ref[h].astype(F32)
        extra = jnp.sum(feat * nin_ref[h][:, :F], axis=1, keepdims=True)
        den = den0_ref[:, columns] + inside * extra
        den_ref[:, columns] = den
        high, low = halves(g_ref[:, columns].astype(F32) / den)
        both = dot((feat * head).astype(BF), jnp.concatenate([high, low], axis=1), (0, 0))
        adj[h] = both[:, :DH] + both[:, DH:]
        return carry

    for c in range(chunks):
        lax.fori_loop(c * CHUNK, (c + 1) * CHUNK, adjoint_of, 0)
        start(1, c, 0)

    weights = {}
    for kind in (0, 1):
        near = before if kind == 0 else after
        for r, b in enumerate(rounds):
            u = lax.rem(me // b, 2)
            own = (me // b) * b
            other = own + b - 2 * b * u
            shift = b - 1 if kind == 0 else 0
            far = doc_at(other + shift, kind)
            w = same(doc_at(own + shift, kind), far)[:, :DH]
            wp = same(far, near)[:, :DH]
            up = (u if kind == 0 else 1 - u).astype(F32)
            keep = up + (1.0 - up) * w
            weights[kind, r] = (up * wp, keep, 1.0 - up, up * w + (1.0 - up))
        base = (me // group) * group
        far = doc_at(base - 1 if kind == 0 else base + group, kind)
        weights[kind, last_round] = same(far, near)[:, :DH]

    def finish(kind, c, r):
        heads = pl.ds(c * CHUNK, CHUNK)
        result = s_ref if kind == 0 else a_ref
        copy = copy_of(kind, c, r)
        if r == last_round:
            @pl.when(can_down if kind == 0 else can_up)
            def _():
                copy.wait_recv()
                result[heads] = result[heads] + weights[kind, r] * got[kind, r, heads]
            return
        copy.wait_recv()
        wp, keep, take, add = weights[kind, r]

        def one(h, carry):
            came = got[kind, r, h]
            if r == 0:
                held = (state_ref if kind == 0 else adj)[h]
                result[h] = wp * came
                suffix[kind, h] = keep * held + take * came
            else:
                held = part[kind, r - 1, h]
                result[h] = result[h] + wp * came
                suffix[kind, h] = keep * suffix[kind, h] + take * came
            if r + 1 < last_round:
                part[kind, r, h] = keep * held + add * came
            return carry

        lax.fori_loop(c * CHUNK, (c + 1) * CHUNK, one, 0)
        start(kind, c, r + 1)

    items = [(kind, c) for kind in (0, 1) for c in range(chunks)]
    for wave in range(len(items) + last_round):
        for r in range(last_round, -1, -1):
            if 0 <= wave - r < len(items):
                finish(*items[wave - r], r)

    for copy in small:
        copy.wait_send()
    for kind, c in items:
        for r in range(last_round):
            copy_of(kind, c, r).wait_send()

        @pl.when(can_up if kind == 0 else can_down)
        def _():
            copy_of(kind, c, last_round).wait_send()


def backward_kernel(
    doc_ref, edge_ref, q_ref, k_ref, v_ref, g_ref, w_ref, fq_ref, probs_ref, s_ref, a_ref, nin_ref, den_ref,
    out_ref, qg_ref, vg_ref, gfk_ref, hn_ref, wg_ref,
):
    tokens = q_ref.shape[0]
    rows = row_docs(doc_ref, (tokens, 1), 0)
    columns = row_docs(doc_ref, (1, tokens), 1)
    mask = jnp.logical_and(
        lax.broadcasted_iota(jnp.int32, (tokens, tokens), 1)
        <= lax.broadcasted_iota(jnp.int32, (tokens, tokens), 0),
        rows == columns,
    )
    inside = same(rows, edge_ref[0:1, :])
    beyond = same(rows, edge_ref[1:2, :])
    inside_f = inside[:, 0:1]
    beyond_f = beyond[:, 0:1]
    head = same(rows, doc_ref[0, 0].astype(F32))
    weight = w_ref[...]
    total = jnp.zeros((DH, F), F32)
    for j in range(STEP):
        part = slice(j * DH, (j + 1) * DH)
        value = v_ref[:, part]
        grad = g_ref[:, part].astype(F32)
        feat_q = fq_ref[j]
        probs = probs_ref[j]
        den = den_ref[:, part]
        proj_q = dot(q_ref[:, part], weight, (1, 0))
        feat_k = features(dot(k_ref[:, part], weight, (1, 0)))
        s_high, s_low = halves(s_ref[j])
        a_high, a_low = halves(a_ref[j])
        carried = dot(feat_q, jnp.concatenate([s_high, s_low], axis=1), (1, 0))
        out = (dot(probs, value, (1, 0)) + inside * (carried[:, :DH] + carried[:, DH:])) / den
        out_ref[:, part] = out
        drift = -jnp.sum(grad * out, axis=1, keepdims=True) / den[:, 0:1]
        line = jnp.sum(feat_q.astype(F32) * (head * drift), axis=0, keepdims=True)
        hn_ref[j] = jnp.concatenate([line, jnp.zeros((1, 256 - F), F32)], axis=1)
        high, low = halves(grad / den)
        dprobs = jnp.where(mask, dot(high, value, (1, 1)) + drift, 0.0).astype(BF)
        cross = dot(
            jnp.concatenate([high, low, high], axis=1),
            jnp.concatenate([s_high, s_high, s_low], axis=1), (1, 1))
        grad_fq = dot(dprobs, feat_k, (1, 0)) + inside_f * (cross + nin_ref[j][:, :F] * drift)
        gfk_ref[j] = dot(dprobs, feat_q, (0, 0)) + beyond_f * dot(
            jnp.concatenate([value, value], axis=1), jnp.concatenate([a_high, a_low], axis=1), (1, 1))
        later = dot(feat_k, jnp.concatenate([a_high, a_low], axis=1), (1, 0))
        vg_ref[:, part] = dot(probs, high, (0, 0)) + beyond * (later[:, :DH] + later[:, DH:])
        grad_pq = (grad_fq * (1.0 + proj_q)).astype(BF)
        qg_ref[:, part] = dot(grad_pq, weight, (1, 1))
        total = total + dot(q_ref[:, part], grad_pq, (0, 0))

    @pl.when(pl.program_id(0) == 0)
    def _():
        wg_ref[...] = total

    @pl.when(pl.program_id(0) > 0)
    def _():
        wg_ref[...] = wg_ref[...] + total


def update_kernel(
    n, dp, group, doc_ref, hn_ref, gfk_ref, k_ref, w_ref, wg_ref,
    kg_ref, new_ref,
    msg, got_msg, drifts, held, got, ms, mr, send, recv,
):
    me = lax.axis_index("ctx")
    row = lax.axis_index("dp")
    hops = [("dp", b) for b in bits(dp)] + [("ctx", b) for b in bits(n)]

    def partner(axis, b):
        at = row if axis == "dp" else me
        return {axis: at + b - 2 * b * lax.rem(at // b, 2)}

    barrier = pltpu.get_barrier_semaphore()
    greeted = 2 * group
    for k in range(1, group + 1):
        for target in (lax.rem(me + k, n), lax.rem(me + n - k, n)):
            pl.semaphore_signal(barrier, inc=1, device_id={"ctx": target}, device_id_type=MESH)
    for axis, b in hops:
        if axis == "dp" or b > group:
            greeted += 1
            pl.semaphore_signal(barrier, inc=1, device_id=partner(axis, b), device_id_type=MESH)

    first = doc_ref[0, 0].astype(F32)
    for h in range(H):
        msg[h : h + 1, :] = hn_ref[h]
    msg[H : H + 8, :] = jnp.broadcast_to(first, (8, 256))
    pl.semaphore_wait(barrier, greeted)
    small = []
    for k in range(1, group + 1):
        small.append(pltpu.make_async_remote_copy(
            src_ref=msg, dst_ref=got_msg.at[k - 1], send_sem=ms.at[k - 1], recv_sem=mr.at[k - 1],
            device_id={"ctx": lax.rem(me + n - k, n)}, device_id_type=MESH))
    for copy in small:
        copy.start()
    for copy in small:
        copy.wait_recv()
    near = got_msg[0, H : H + 1, :]
    norm = jnp.zeros((H, 256), F32)
    for k in range(1, group + 1):
        w = same(got_msg[k - 1, H : H + 1, :], near) * jnp.where(me + k < n, 1.0, 0.0)
        norm = norm + w * got_msg[k - 1, 0:H, :]
    for h in range(H):
        drifts[h] = norm[h : h + 1, :]
    tokens = k_ref.shape[0]
    beyond = same(row_docs(doc_ref, (tokens, 1), 0), near)[:, :F]
    weight = w_ref[...]

    def one(h, total):
        columns = head_columns(h)
        key = k_ref[:, columns]
        grad_fk = gfk_ref[h] + beyond * drifts[h][:, :F]
        grad_pk = (grad_fk * (1.0 + dot(key, weight, (1, 0)))).astype(BF)
        kg_ref[:, columns] = dot(grad_pk, weight, (1, 1))
        return total + dot(key, grad_pk, (0, 0))

    total = lax.fori_loop(0, H, one, wg_ref[...])
    copies = []
    for r, (axis, b) in enumerate(hops):
        held[r] = total
        copy = pltpu.make_async_remote_copy(
            src_ref=held.at[r], dst_ref=got.at[r], send_sem=send.at[r], recv_sem=recv.at[r],
            device_id=partner(axis, b), device_id_type=MESH)
        copy.start()
        copy.wait_recv()
        copies.append(copy)
        total = total + got[r]
    scale = lax.rsqrt(jnp.sum(total * total, keepdims=True) / (DH * F) + EPSILON)
    new_ref[...] = weight.astype(F32) - RATE * total * scale
    for copy in small + copies:
        copy.wait_send()


def shards(n, dp, queries, keys, values, doc_ids, feat_weight, out_grad):
    tokens = queries.shape[1]
    wide = H * DH
    group = max(1, n // 4)
    q, k, v, g = (x.reshape(tokens, wide) for x in (queries, keys, values, out_grad))
    shape = jax.ShapeDtypeStruct
    smem = pl.BlockSpec(memory_space=pltpu.SMEM)
    vmem = pl.BlockSpec(memory_space=pltpu.VMEM)
    cols = pl.BlockSpec((tokens, STEP * DH), lambda i: (0, i))
    whole = pl.BlockSpec((DH, F), lambda i: (0, 0))

    def per_head(*dims):
        return pl.BlockSpec((STEP,) + dims, lambda i: (i, 0, 0))

    feat_q, probs, state, norm, den0 = pl.pallas_call(
        local_kernel,
        grid=(H // STEP,),
        in_specs=[smem, cols, cols, cols, whole],
        out_specs=[per_head(tokens, F), per_head(tokens, tokens), per_head(F, DH), per_head(1, 256), cols],
        out_shape=[
            shape((H, tokens, F), BF), shape((H, tokens, tokens), BF), shape((H, F, DH), F32),
            shape((H, 1, 256), F32), shape((tokens, wide), F32),
        ],
        compiler_params=pltpu.CompilerParams(vmem_limit_bytes=LIMIT),
    )(doc_ids, q, k, v, feat_weight)

    rounds = len(bits(group))
    slots = 2 * (H // CHUNK) * (rounds + 1)
    dma = pltpu.SemaphoreType.DMA
    state_in, adjoint, norm_in, den, edge = pl.pallas_call(
        functools.partial(exchange_kernel, n, group),
        in_specs=[smem] + [vmem] * 5,
        out_specs=[vmem] * 5,
        out_shape=[
            shape((H, F, DH), F32), shape((H, F, DH), F32), shape((H, 1, 256), F32),
            shape((tokens, wide), F32), shape((8, DH), F32),
        ],
        scratch_shapes=[
            pltpu.VMEM((H + 8, 256), F32),
            pltpu.VMEM((8, 256), F32),
            pltpu.VMEM((2 * group + 1, 8, 256), F32),
            pltpu.VMEM((group, H + 8, 256), F32),
            pltpu.VMEM((group, 8, 256), F32),
            pltpu.VMEM((H, F, DH), F32),
            pltpu.VMEM((2, max(1, rounds - 1), H, F, DH), F32),
            pltpu.VMEM((2, H, F, DH), F32),
            pltpu.VMEM((2, rounds + 1, H, F, DH), F32),
            dma((group,)), dma((group,)), dma((group,)), dma((group,)), dma((slots,)), dma((slots,)),
        ],
        compiler_params=pltpu.CompilerParams(
            collective_id=0, has_side_effects=True, vmem_limit_bytes=LIMIT),
    )(doc_ids, feat_q, state, norm, den0, g)

    out, query_grad, value_grad, grad_fk, head_norm, weight_q = pl.pallas_call(
        backward_kernel,
        grid=(H // STEP,),
        in_specs=[
            smem, pl.BlockSpec((8, DH), lambda i: (0, 0)), cols, cols, cols, cols, whole,
            per_head(tokens, F), per_head(tokens, tokens), per_head(F, DH), per_head(F, DH),
            per_head(1, 256), cols,
        ],
        out_specs=[cols, cols, cols, per_head(tokens, F), per_head(1, 256), whole],
        out_shape=[shape((tokens, wide), F32)] * 3 + [
            shape((H, tokens, F), F32), shape((H, 1, 256), F32), shape((DH, F), F32)],
        compiler_params=pltpu.CompilerParams(vmem_limit_bytes=LIMIT),
    )(doc_ids, edge, q, k, v, g, feat_weight, feat_q, probs, state_in, adjoint, norm_in, den)

    steps = len(bits(n)) + len(bits(dp))
    key_grad, new_weight = pl.pallas_call(
        functools.partial(update_kernel, n, dp, group),
        in_specs=[smem] + [vmem] * 5,
        out_specs=[vmem] * 2,
        out_shape=[shape((tokens, wide), F32), shape((DH, F), F32)],
        scratch_shapes=[
            pltpu.VMEM((H + 8, 256), F32),
            pltpu.VMEM((group, H + 8, 256), F32),
            pltpu.VMEM((H, 1, 256), F32),
            pltpu.VMEM((steps, DH, F), F32),
            pltpu.VMEM((steps, DH, F), F32),
            dma((group,)), dma((group,)), dma((steps,)), dma((steps,)),
        ],
        compiler_params=pltpu.CompilerParams(
            collective_id=1, has_side_effects=True, vmem_limit_bytes=LIMIT),
    )(doc_ids, head_norm, grad_fk, k, feat_weight, weight_q)

    full = (1, tokens, wide)
    return (
        out.reshape(full), query_grad.reshape(full), key_grad.reshape(full), value_grad.reshape(full),
        new_weight,
    )


def solution(mesh):
    split = P("dp", "ctx", None)
    return jax.shard_map(
        functools.partial(shards, mesh.shape["ctx"], mesh.shape["dp"]),
        mesh=mesh,
        in_specs=(split, split, split, P("dp", "ctx"), P(), split),
        out_specs=(split, split, split, split, P()),
        check_vma=False,
    )
```

```python
import functools

import jax
import jax.numpy as jnp
from jax import lax
from jax.experimental import pallas as pl
from jax.experimental.pallas import tpu as pltpu
from jax.sharding import PartitionSpec as P

H = 16
DH = 128
F = 160
BLOCK = 64
RATE = 0.5
EPSILON = 1e-06
CHUNK = 2
LAG = 2
MESH = pl.DeviceIdType.MESH
BF = jnp.bfloat16
F32 = jnp.float32
LIMIT = 56 * 1024 * 1024


def dot(a, b, dims):
    return lax.dot_general(a, b, ((dims[:1], dims[1:]), ((), ())), preferred_element_type=F32)


def features(proj):
    return (1.0 + proj + 0.5 * proj * proj).astype(BF)


def halves(x):
    high = x.astype(BF)
    return high, (x - high.astype(F32)).astype(BF)


def row_docs(doc_ref, shape, dim):
    place = lax.broadcasted_iota(jnp.int32, shape, dim) // BLOCK
    docs = jnp.zeros(shape, F32)
    for block in range(doc_ref.shape[1]):
        docs = jnp.where(place == block, doc_ref[0, block].astype(F32), docs)
    return docs


def same(a, b):
    return jnp.where(a == b, 1.0, 0.0)


def bits(count):
    return [1 << r for r in range(count.bit_length() - 1)]


def kernel(
    n, dp, group, doc_ref, q_ref, k_ref, v_ref, g_ref, w_ref,
    out_ref, qg_ref, kg_ref, vg_ref, new_ref,
    fq, fk, probs_s, den_s, s_s, a_s, nin_s, hn_s, drift_s,
    msg, note, table, got_msg, got_note, hmsg, got_hmsg,
    own_sum, part, suffix, got, acc, held, got_w, got_half, got_final,
    ms, mr, ns, nr, hs, hr, send, recv, wsend, wrecv,
):
    me = lax.axis_index("ctx")
    row = lax.axis_index("dp")
    tokens = q_ref.shape[0]
    rounds = bits(group)
    last_round = len(rounds)
    chunks = H // CHUNK
    hops = bits(n)

    def partner(b):
        return {"ctx": me + b - 2 * b * lax.rem(me // b, 2)}

    other_core = {"dp": 1 - row}

    barrier = pltpu.get_barrier_semaphore()
    greeted = 2 * group + 1
    for k in range(1, group + 1):
        for target in (lax.rem(me + k, n), lax.rem(me + n - k, n)):
            pl.semaphore_signal(barrier, inc=1, device_id={"ctx": target}, device_id_type=MESH)
    pl.semaphore_signal(barrier, inc=1, device_id=other_core, device_id_type=MESH)
    for b in hops:
        if b > group:
            greeted += 1
            pl.semaphore_signal(barrier, inc=1, device_id=partner(b), device_id_type=MESH)

    last = doc_ref[0, doc_ref.shape[1] - 1].astype(F32)
    first = doc_ref[0, 0].astype(F32)
    which = lax.broadcasted_iota(jnp.int32, (8, 256), 0)
    tile = jnp.where(which == 0, last, jnp.where(which == 1, first, 0.0))
    note[...] = tile
    table[group] = tile
    msg[H : H + 8, :] = tile
    hmsg[H : H + 8, :] = tile
    rows = row_docs(doc_ref, (tokens, 1), 0)
    mask = jnp.logical_and(
        lax.broadcasted_iota(jnp.int32, (tokens, tokens), 1)
        <= lax.broadcasted_iota(jnp.int32, (tokens, tokens), 0),
        rows == row_docs(doc_ref, (1, tokens), 1),
    )
    tail = same(rows, last)
    head = same(rows, first)
    weight = w_ref[...]
    ones = jnp.ones((tokens, DH), BF)
    zeros = jnp.zeros((1, 256 - F), F32)

    def heads_of(c):
        return range(c * CHUNK, (c + 1) * CHUNK)

    def columns(h):
        return slice(h * DH, (h + 1) * DH)

    def copy_of(kind, c, r):
        heads = pl.ds(c * CHUNK, CHUNK)
        if r < last_round:
            target = partner(rounds[r])
        else:
            target = {"ctx": me + group if kind == 0 else me - group}
        if r == 0:
            source = own_sum.at[kind, heads]
        elif r < last_round:
            source = part.at[kind, r - 1, heads]
        else:
            source = suffix.at[kind, heads]
        slot = (kind * chunks + c) * (last_round + 1) + r
        return pltpu.make_async_remote_copy(
            src_ref=source, dst_ref=got.at[kind, r, heads], send_sem=send.at[slot], recv_sem=recv.at[slot],
            device_id=target, device_id_type=MESH)

    can_up = me + group < n
    can_down = me >= group

    def start(kind, c, r):
        if r < last_round:
            copy_of(kind, c, r).start()
        else:
            @pl.when(can_up if kind == 0 else can_down)
            def _():
                copy_of(kind, c, r).start()

    for c in range(chunks):
        for h in heads_of(c):
            feat = features(dot(k_ref[:, columns(h)], weight, (1, 0)))
            fk[h] = feat
            tail_k = feat.astype(F32) * tail
            own_sum[0, h] = dot(tail_k.astype(BF), v_ref[:, columns(h)], (0, 0))
            line = jnp.sum(tail_k, axis=0, keepdims=True)
            msg[h : h + 1, :] = jnp.concatenate([line, zeros], axis=1)
        if c == 0:
            pl.semaphore_wait(barrier, greeted)
        start(0, c, 0)

    small = []
    for k in range(1, group + 1):
        small.append(pltpu.make_async_remote_copy(
            src_ref=msg, dst_ref=got_msg.at[k - 1], send_sem=ms.at[k - 1], recv_sem=mr.at[k - 1],
            device_id={"ctx": lax.rem(me + k, n)}, device_id_type=MESH))
        small.append(pltpu.make_async_remote_copy(
            src_ref=note, dst_ref=got_note.at[k - 1], send_sem=ns.at[k - 1], recv_sem=nr.at[k - 1],
            device_id={"ctx": lax.rem(me + n - k, n)}, device_id_type=MESH))
    for copy in small:
        copy.start()

    def scores(c):
        for h in heads_of(c):
            feat_q = features(dot(q_ref[:, columns(h)], weight, (1, 0)))
            probs = jnp.where(mask, dot(feat_q, fk[h], (1, 1)), 0.0).astype(BF)
            fq[h] = feat_q
            probs_s[h] = probs
            den_s[:, columns(h)] = dot(probs, ones, (1, 0))

    scores(0)
    scores(1)
    for copy in small:
        copy.wait_recv()
    for k in range(1, group + 1):
        table[group - k] = got_msg[k - 1, H : H + 8, :]
        table[group + k] = got_note[k - 1]

    def doc_at(index, kind):
        return table[index - me + group][kind : kind + 1, :]

    before = table[group - 1][0:1, :]
    after = table[group + 1][1:2, :]
    norm = jnp.zeros((H, 256), F32)
    for k in range(1, group + 1):
        w = same(got_msg[k - 1, H : H + 1, :], before) * jnp.where(me >= k, 1.0, 0.0)
        norm = norm + w * got_msg[k - 1, 0:H, :]
    nin_s[...] = norm
    inside = same(rows, before[:, :DH])
    beyond = same(rows, after[:, :DH])
    inside_f = inside[:, 0:1]
    beyond_f = beyond[:, 0:1]

    def adjoint(c):
        for h in heads_of(c):
            feat = fq[h].astype(F32)
            extra = jnp.sum(feat * nin_s[h : h + 1, :F], axis=1, keepdims=True)
            den = den_s[:, columns(h)] + inside * extra
            den_s[:, columns(h)] = den
            high, low = halves(g_ref[:, columns(h)].astype(F32) / den)
            both = dot((feat * head).astype(BF), jnp.concatenate([high, low], axis=1), (0, 0))
            own_sum[1, h] = both[:, :DH] + both[:, DH:]

    weights = {}
    for kind in (0, 1):
        near = before if kind == 0 else after
        for r, b in enumerate(rounds):
            u = lax.rem(me // b, 2)
            own = (me // b) * b
            other = own + b - 2 * b * u
            shift = b - 1 if kind == 0 else 0
            far = doc_at(other + shift, kind)
            w = same(doc_at(own + shift, kind), far)[:, :DH]
            wp = same(far, near)[:, :DH]
            up = (u if kind == 0 else 1 - u).astype(F32)
            keep = up + (1.0 - up) * w
            weights[kind, r] = (up * wp, keep, 1.0 - up, up * w + (1.0 - up))
        base = (me // group) * group
        far = doc_at(base - 1 if kind == 0 else base + group, kind)
        weights[kind, last_round] = same(far, near)[:, :DH]

    def finish(kind, c, r):
        heads = pl.ds(c * CHUNK, CHUNK)
        result = s_s if kind == 0 else a_s
        copy = copy_of(kind, c, r)
        if r == last_round:
            @pl.when(can_down if kind == 0 else can_up)
            def _():
                copy.wait_recv()
                result[heads] = result[heads] + weights[kind, r] * got[kind, r, heads]
            return
        copy.wait_recv()
        wp, keep, take, add = weights[kind, r]
        for h in heads_of(c):
            came = got[kind, r, h]
            if r == 0:
                mine = own_sum[kind, h]
                result[h] = wp * came
                suffix[kind, h] = keep * mine + take * came
            else:
                mine = part[kind, r - 1, h]
                result[h] = result[h] + wp * came
                suffix[kind, h] = keep * suffix[kind, h] + take * came
            if r + 1 < last_round:
                part[kind, r, h] = keep * mine + add * came
        start(kind, c, r + 1)

    def query_side(c, total):
        for h in heads_of(c):
            grad = g_ref[:, columns(h)].astype(F32)
            feat_q = fq[h]
            den = den_s[:, columns(h)]
            value = v_ref[:, columns(h)]
            query = q_ref[:, columns(h)]
            s_high, s_low = halves(s_s[h])
            carried = dot(feat_q, jnp.concatenate([s_high, s_low], axis=1), (1, 0))
            out = (dot(probs_s[h], value, (1, 0)) + inside * (carried[:, :DH] + carried[:, DH:])) / den
            out_ref[:, columns(h)] = out
            drift = -jnp.sum(grad * out, axis=1, keepdims=True) / den[:, 0:1]
            line = jnp.sum(feat_q.astype(F32) * (head * drift), axis=0, keepdims=True)
            hmsg[h : h + 1, :] = jnp.concatenate([line, zeros], axis=1)
            high, low = halves(grad / den)
            dprobs = jnp.where(mask, dot(high, value, (1, 1)) + drift, 0.0).astype(BF)
            cross = dot(
                jnp.concatenate([high, low, high], axis=1),
                jnp.concatenate([s_high, s_high, s_low], axis=1), (1, 1))
            grad_fq = dot(dprobs, fk[h], (1, 0)) + inside_f * (cross + nin_s[h : h + 1, :F] * drift)
            hn_s[h] = dot(dprobs, feat_q, (0, 0))
            vg_ref[:, columns(h)] = dot(probs_s[h], high, (0, 0))
            grad_pq = (grad_fq * (1.0 + dot(query, weight, (1, 0)))).astype(BF)
            qg_ref[:, columns(h)] = dot(grad_pq, weight, (1, 1))
            total = total + dot(grad_pq, query, (0, 0))
        return total

    def key_side(c, total):
        for h in heads_of(c):
            value = v_ref[:, columns(h)]
            key = k_ref[:, columns(h)]
            split = jnp.concatenate(halves(a_s[h]), axis=1)
            later = dot(fk[h], split, (1, 0))
            vg_ref[:, columns(h)] = vg_ref[:, columns(h)] + beyond * (later[:, :DH] + later[:, DH:])
            from_later = dot(jnp.concatenate([value, value], axis=1), split, (1, 1))
            grad_fk = hn_s[h] + beyond_f * (from_later + drift_s[h : h + 1, :F])
            grad_pk = (grad_fk * (1.0 + dot(key, weight, (1, 0)))).astype(BF)
            kg_ref[:, columns(h)] = dot(grad_pk, weight, (1, 1))
            total = total + dot(grad_pk, key, (0, 0))
        return total

    drifts = []
    for k in range(1, group + 1):
        drifts.append(pltpu.make_async_remote_copy(
            src_ref=hmsg, dst_ref=got_hmsg.at[k - 1], send_sem=hs.at[k - 1], recv_sem=hr.at[k - 1],
            device_id={"ctx": lax.rem(me + n - k, n)}, device_id_type=MESH))

    def take_drifts():
        for copy in drifts:
            copy.wait_recv()
        norm = jnp.zeros((H, 256), F32)
        for k in range(1, group + 1):
            w = same(got_hmsg[k - 1, H + 1 : H + 2, :], after) * jnp.where(me + k < n, 1.0, 0.0)
            norm = norm + w * got_hmsg[k - 1, 0:H, :]
        drift_s[...] = norm

    items = [(kind, c) for kind in (0, 1) for c in range(chunks)]
    drain = LAG * last_round
    key_from = chunks + drain + 1
    total = jnp.zeros((F, DH), F32)
    keys_done = 0
    for wave in range(len(items) + drain):
        for r in range(last_round + 1):
            if 0 <= wave - LAG * r < len(items):
                finish(*items[wave - LAG * r], r)
        if wave < chunks:
            if 2 <= wave + 2 < chunks:
                scores(wave + 2)
            adjoint(wave)
            start(1, wave, 0)
        if 0 <= wave - drain < chunks:
            total = query_side(wave - drain, total)
        if wave - drain == chunks - 1:
            for copy in drifts:
                copy.start()
        if wave == key_from:
            take_drifts()
        if wave >= key_from:
            while keys_done <= wave - drain - chunks and keys_done < chunks:
                total = key_side(keys_done, total)
                keys_done += 1
    assert keys_done == chunks

    half = F // dp
    acc[...] = total
    mine = pl.ds(row * half, half)
    theirs = pl.ds((1 - row) * half, half)
    sums = [pltpu.make_async_remote_copy(
        src_ref=acc.at[theirs], dst_ref=got_half, send_sem=wsend.at[0], recv_sem=wrecv.at[0],
        device_id=other_core, device_id_type=MESH)]
    sums[0].start()
    sums[0].wait_recv()
    total = acc[mine] + got_half[...]
    for r, b in enumerate(hops):
        held[r] = total
        copy = pltpu.make_async_remote_copy(
            src_ref=held.at[r], dst_ref=got_w.at[r], send_sem=wsend.at[r + 1], recv_sem=wrecv.at[r + 1],
            device_id=partner(b), device_id_type=MESH)
        copy.start()
        copy.wait_recv()
        sums.append(copy)
        total = total + got_w[r]
    steps = len(hops)
    held[steps] = total
    copy = pltpu.make_async_remote_copy(
        src_ref=held.at[steps], dst_ref=got_final, send_sem=wsend.at[steps + 1], recv_sem=wrecv.at[steps + 1],
        device_id=other_core, device_id_type=MESH)
    copy.start()
    sums.append(copy)
    copy.wait_recv()
    for copy in sums:
        copy.wait_send()
    acc[mine] = total
    acc[theirs] = got_final[...]
    whole = acc[...]
    scale = lax.rsqrt(jnp.sum(whole * whole, keepdims=True) / (DH * F) + EPSILON)
    new_ref[...] = weight.astype(F32) - jnp.transpose(RATE * whole * scale)

    for copy in small + drifts:
        copy.wait_send()
    for kind, c in items:
        for r in range(last_round):
            copy_of(kind, c, r).wait_send()

        @pl.when(can_up if kind == 0 else can_down)
        def _():
            copy_of(kind, c, last_round).wait_send()


def shards(n, dp, queries, keys, values, doc_ids, feat_weight, out_grad):
    tokens = queries.shape[1]
    wide = H * DH
    group = max(2, n // 4)
    q, k, v, g = (x.reshape(tokens, wide) for x in (queries, keys, values, out_grad))
    rounds = len(bits(group))
    steps = len(bits(n))
    slots = 2 * (H // CHUNK) * (rounds + 1)
    shape = jax.ShapeDtypeStruct
    vmem = pl.BlockSpec(memory_space=pltpu.VMEM)
    dma = pltpu.SemaphoreType.DMA
    results = pl.pallas_call(
        functools.partial(kernel, n, dp, group),
        in_specs=[pl.BlockSpec(memory_space=pltpu.SMEM)] + [vmem] * 5,
        out_specs=[vmem] * 5,
        out_shape=[shape((tokens, wide), F32)] * 4 + [shape((DH, F), F32)],
        scratch_shapes=[
            pltpu.VMEM((H, tokens, F), BF),
            pltpu.VMEM((H, tokens, F), BF),
            pltpu.VMEM((H, tokens, tokens), BF),
            pltpu.VMEM((tokens, wide), F32),
            pltpu.VMEM((H, F, DH), F32),
            pltpu.VMEM((H, F, DH), F32),
            pltpu.VMEM((H, 256), F32),
            pltpu.VMEM((H, tokens, F), F32),
            pltpu.VMEM((H, 256), F32),
            pltpu.VMEM((H + 8, 256), F32),
            pltpu.VMEM((8, 256), F32),
            pltpu.VMEM((2 * group + 1, 8, 256), F32),
            pltpu.VMEM((group, H + 8, 256), F32),
            pltpu.VMEM((group, 8, 256), F32),
            pltpu.VMEM((H + 8, 256), F32),
            pltpu.VMEM((group, H + 8, 256), F32),
            pltpu.VMEM((2, H, F, DH), F32),
            pltpu.VMEM((2, max(1, rounds - 1), H, F, DH), F32),
            pltpu.VMEM((2, H, F, DH), F32),
            pltpu.VMEM((2, rounds + 1, H, F, DH), F32),
            pltpu.VMEM((F, DH), F32),
            pltpu.VMEM((steps + 1, F // dp, DH), F32),
            pltpu.VMEM((steps, F // dp, DH), F32),
            pltpu.VMEM((F // dp, DH), F32),
            pltpu.VMEM((F // dp, DH), F32),
            dma((group,)), dma((group,)), dma((group,)), dma((group,)), dma((group,)), dma((group,)),
            dma((slots,)), dma((slots,)), dma((steps + 2,)), dma((steps + 2,)),
        ],
        compiler_params=pltpu.CompilerParams(
            collective_id=0, has_side_effects=True, vmem_limit_bytes=LIMIT),
    )(doc_ids, q, k, v, g, feat_weight)
    full = (1, tokens, wide)
    return tuple(x.reshape(full) for x in results[:4]) + (results[4],)


def solution(mesh):
    split = P("dp", "ctx", None)
    return jax.shard_map(
        functools.partial(shards, mesh.shape["ctx"], mesh.shape["dp"]),
        mesh=mesh,
        in_specs=(split, split, split, P("dp", "ctx"), P(), split),
        out_specs=(split, split, split, split, P()),
        check_vma=False,
    )
```

```python
import functools

import jax
import jax.numpy as jnp
from jax import lax
from jax.experimental import pallas as pl
from jax.experimental.pallas import tpu as pltpu
from jax.sharding import PartitionSpec as P

H = 16
DH = 128
F = 160
BLOCK = 64
RATE = 0.5
EPSILON = 1e-06
CHUNK = 2
LAG = 2
AHEAD = 3
MESH = pl.DeviceIdType.MESH
BF = jnp.bfloat16
F32 = jnp.float32
LIMIT = 56 * 1024 * 1024


def dot(a, b, dims):
    return lax.dot_general(a, b, ((dims[:1], dims[1:]), ((), ())), preferred_element_type=F32)


def features(proj):
    return (1.0 + proj + 0.5 * proj * proj).astype(BF)


def halves(x):
    high = x.astype(BF)
    return high, (x - high.astype(F32)).astype(BF)


def row_docs(doc_ref, shape, dim):
    place = lax.broadcasted_iota(jnp.int32, shape, dim) // BLOCK
    docs = jnp.zeros(shape, F32)
    for block in range(doc_ref.shape[1]):
        docs = jnp.where(place == block, doc_ref[0, block].astype(F32), docs)
    return docs


def same(a, b):
    return jnp.where(a == b, 1.0, 0.0)


def bits(count):
    return [1 << r for r in range(count.bit_length() - 1)]


def kernel(
    n, dp, group, doc_ref, q_ref, k_ref, v_ref, g_ref, w_ref,
    out_ref, qg_ref, kg_ref, vg_ref, new_ref,
    fq, fk, probs_s, den_s, s_s, a_s, nin_s, hn_s, drift_s,
    msg, note, table, got_msg, got_note, hmsg, got_hmsg,
    own_sum, part, suffix, got, acc, held, got_w, got_half, got_final,
    ms, mr, ns, nr, hs, hr, send, recv, wsend, wrecv,
):
    me = lax.axis_index("ctx")
    row = lax.axis_index("dp")
    tokens = q_ref.shape[0]
    rounds = bits(group)
    last_round = len(rounds)
    chunks = H // CHUNK
    hops = bits(n)

    def partner(b):
        return {"ctx": me + b - 2 * b * lax.rem(me // b, 2)}

    other_core = {"dp": 1 - row}

    barrier = pltpu.get_barrier_semaphore()
    greeted = 2 * group + 1
    for k in range(1, group + 1):
        for target in (lax.rem(me + k, n), lax.rem(me + n - k, n)):
            pl.semaphore_signal(barrier, inc=1, device_id={"ctx": target}, device_id_type=MESH)
    pl.semaphore_signal(barrier, inc=1, device_id=other_core, device_id_type=MESH)
    for b in hops:
        if b > group:
            greeted += 1
            pl.semaphore_signal(barrier, inc=1, device_id=partner(b), device_id_type=MESH)

    last = doc_ref[0, doc_ref.shape[1] - 1].astype(F32)
    first = doc_ref[0, 0].astype(F32)
    which = lax.broadcasted_iota(jnp.int32, (8, 256), 0)
    tile = jnp.where(which == 0, last, jnp.where(which == 1, first, 0.0))
    note[...] = tile
    table[group] = tile
    msg[H : H + 8, :] = tile
    hmsg[H : H + 8, :] = tile
    rows = row_docs(doc_ref, (tokens, 1), 0)
    mask = jnp.logical_and(
        lax.broadcasted_iota(jnp.int32, (tokens, tokens), 1)
        <= lax.broadcasted_iota(jnp.int32, (tokens, tokens), 0),
        rows == row_docs(doc_ref, (1, tokens), 1),
    )
    tail = same(rows, last)
    head = same(rows, first)
    weight = w_ref[...]
    ones = jnp.ones((tokens, DH), BF)
    zeros = jnp.zeros((1, 256 - F), F32)

    def heads_of(c):
        return range(c * CHUNK, (c + 1) * CHUNK)

    def columns(h):
        return slice(h * DH, (h + 1) * DH)

    def copy_of(kind, c, r):
        heads = pl.ds(c * CHUNK, CHUNK)
        if r < last_round:
            target = partner(rounds[r])
        else:
            target = {"ctx": me + group if kind == 0 else me - group}
        if r == 0:
            source = own_sum.at[kind, heads]
        elif r < last_round:
            source = part.at[kind, r - 1, heads]
        else:
            source = suffix.at[kind, heads]
        slot = (kind * chunks + c) * (last_round + 1) + r
        return pltpu.make_async_remote_copy(
            src_ref=source, dst_ref=got.at[kind, r, heads], send_sem=send.at[slot], recv_sem=recv.at[slot],
            device_id=target, device_id_type=MESH)

    can_up = me + group < n
    can_down = me >= group

    def start(kind, c, r):
        if r < last_round:
            copy_of(kind, c, r).start()
        else:
            @pl.when(can_up if kind == 0 else can_down)
            def _():
                copy_of(kind, c, r).start()

    for h in range(H):
        feat = features(dot(k_ref[:, columns(h)], weight, (1, 1)))
        fk[h] = feat
        line = jnp.sum(feat.astype(F32) * tail, axis=0, keepdims=True)
        msg[h : h + 1, :] = jnp.concatenate([line, zeros], axis=1)
    pl.semaphore_wait(barrier, greeted)

    small = []
    for k in range(1, group + 1):
        small.append(pltpu.make_async_remote_copy(
            src_ref=msg, dst_ref=got_msg.at[k - 1], send_sem=ms.at[k - 1], recv_sem=mr.at[k - 1],
            device_id={"ctx": lax.rem(me + k, n)}, device_id_type=MESH))
        small.append(pltpu.make_async_remote_copy(
            src_ref=note, dst_ref=got_note.at[k - 1], send_sem=ns.at[k - 1], recv_sem=nr.at[k - 1],
            device_id={"ctx": lax.rem(me + n - k, n)}, device_id_type=MESH))
    for copy in small:
        copy.start()
    for c in range(chunks):
        for h in heads_of(c):
            tail_k = (fk[h].astype(F32) * tail).astype(BF)
            own_sum[0, h] = dot(tail_k, v_ref[:, columns(h)], (0, 0))
        if c < AHEAD:
            start(0, c, 0)

    def scores(c):
        for h in heads_of(c):
            feat_q = features(dot(q_ref[:, columns(h)], weight, (1, 1)))
            probs = jnp.where(mask, dot(feat_q, fk[h], (1, 1)), 0.0).astype(BF)
            fq[h] = feat_q
            probs_s[h] = probs
            den_s[:, columns(h)] = dot(probs, ones, (1, 0))

    scores(0)
    scores(1)
    for copy in small:
        copy.wait_recv()
    for k in range(1, group + 1):
        table[group - k] = got_msg[k - 1, H : H + 8, :]
        table[group + k] = got_note[k - 1]

    def doc_at(index, kind):
        return table[index - me + group][kind : kind + 1, :]

    before = table[group - 1][0:1, :]
    after = table[group + 1][1:2, :]
    norm = jnp.zeros((H, 256), F32)
    for k in range(1, group + 1):
        w = same(got_msg[k - 1, H : H + 1, :], before) * jnp.where(me >= k, 1.0, 0.0)
        norm = norm + w * got_msg[k - 1, 0:H, :]
    nin_s[...] = norm
    inside = same(rows, before[:, :DH])
    beyond = same(rows, after[:, :DH])
    inside_f = inside[:, 0:1]
    beyond_f = beyond[:, 0:1]

    def adjoint(c):
        for h in heads_of(c):
            feat = fq[h].astype(F32)
            extra = jnp.sum(feat * nin_s[h : h + 1, :F], axis=1, keepdims=True)
            den = den_s[:, columns(h)] + inside * extra
            den_s[:, columns(h)] = den
            high, low = halves(g_ref[:, columns(h)].astype(F32) / den)
            both = dot((feat * head).astype(BF), jnp.concatenate([high, low], axis=1), (0, 0))
            own_sum[1, h] = both[:, :DH] + both[:, DH:]

    weights = {}
    for kind in (0, 1):
        near = before if kind == 0 else after
        for r, b in enumerate(rounds):
            u = lax.rem(me // b, 2)
            own = (me // b) * b
            other = own + b - 2 * b * u
            shift = b - 1 if kind == 0 else 0
            far = doc_at(other + shift, kind)
            w = same(doc_at(own + shift, kind), far)[:, :DH]
            wp = same(far, near)[:, :DH]
            up = (u if kind == 0 else 1 - u).astype(F32)
            keep = up + (1.0 - up) * w
            weights[kind, r] = (up * wp, keep, 1.0 - up, up * w + (1.0 - up))
        base = (me // group) * group
        far = doc_at(base - 1 if kind == 0 else base + group, kind)
        weights[kind, last_round] = same(far, near)[:, :DH]

    def finish(kind, c, r):
        heads = pl.ds(c * CHUNK, CHUNK)
        result = s_s if kind == 0 else a_s
        copy = copy_of(kind, c, r)
        if r == last_round:
            @pl.when(can_down if kind == 0 else can_up)
            def _():
                copy.wait_recv()
                result[heads] = result[heads] + weights[kind, r] * got[kind, r, heads]
            return
        copy.wait_recv()
        wp, keep, take, add = weights[kind, r]
        for h in heads_of(c):
            came = got[kind, r, h]
            if r == 0:
                mine = own_sum[kind, h]
                result[h] = wp * came
                suffix[kind, h] = keep * mine + take * came
            else:
                mine = part[kind, r - 1, h]
                result[h] = result[h] + wp * came
                suffix[kind, h] = keep * suffix[kind, h] + take * came
            if r + 1 < last_round:
                part[kind, r, h] = keep * mine + add * came
        start(kind, c, r + 1)

    def query_side(c, total):
        for h in heads_of(c):
            grad = g_ref[:, columns(h)].astype(F32)
            feat_q = fq[h]
            den = den_s[:, columns(h)]
            value = v_ref[:, columns(h)]
            query = q_ref[:, columns(h)]
            s_high, s_low = halves(s_s[h])
            carried = dot(feat_q, jnp.concatenate([s_high, s_low], axis=1), (1, 0))
            out = (dot(probs_s[h], value, (1, 0)) + inside * (carried[:, :DH] + carried[:, DH:])) / den
            out_ref[:, columns(h)] = out
            drift = -jnp.sum(grad * out, axis=1, keepdims=True) / den[:, 0:1]
            line = jnp.sum(feat_q.astype(F32) * (head * drift), axis=0, keepdims=True)
            hmsg[h : h + 1, :] = jnp.concatenate([line, zeros], axis=1)
            high, low = halves(grad / den)
            dprobs = jnp.where(mask, dot(high, value, (1, 1)) + drift, 0.0).astype(BF)
            cross = dot(
                jnp.concatenate([high, low, high], axis=1),
                jnp.concatenate([s_high, s_high, s_low], axis=1), (1, 1))
            grad_fq = dot(dprobs, fk[h], (1, 0)) + inside_f * (cross + nin_s[h : h + 1, :F] * drift)
            hn_s[h] = dot(dprobs, feat_q, (0, 0))
            vg_ref[:, columns(h)] = dot(probs_s[h], high, (0, 0))
            grad_pq = (grad_fq * (1.0 + dot(query, weight, (1, 1)))).astype(BF)
            qg_ref[:, columns(h)] = dot(grad_pq, weight, (1, 0))
            total = total + dot(grad_pq, query, (0, 0))
        return total

    def key_first(c):
        for h in heads_of(c):
            value = v_ref[:, columns(h)]
            split = jnp.concatenate(halves(a_s[h]), axis=1)
            later = dot(fk[h], split, (1, 0))
            vg_ref[:, columns(h)] = vg_ref[:, columns(h)] + beyond * (later[:, :DH] + later[:, DH:])
            from_later = dot(jnp.concatenate([value, value], axis=1), split, (1, 1))
            hn_s[h] = hn_s[h] + beyond_f * from_later

    def key_side(c, total):
        for h in heads_of(c):
            key = k_ref[:, columns(h)]
            grad_fk = hn_s[h] + beyond_f * drift_s[h : h + 1, :F]
            grad_pk = (grad_fk * (1.0 + dot(key, weight, (1, 1)))).astype(BF)
            kg_ref[:, columns(h)] = dot(grad_pk, weight, (1, 0))
            total = total + dot(grad_pk, key, (0, 0))
        return total

    drifts = []
    for k in range(1, group + 1):
        drifts.append(pltpu.make_async_remote_copy(
            src_ref=hmsg, dst_ref=got_hmsg.at[k - 1], send_sem=hs.at[k - 1], recv_sem=hr.at[k - 1],
            device_id={"ctx": lax.rem(me + n - k, n)}, device_id_type=MESH))

    def take_drifts():
        for copy in drifts:
            copy.wait_recv()
        norm = jnp.zeros((H, 256), F32)
        for k in range(1, group + 1):
            w = same(got_hmsg[k - 1, H + 1 : H + 2, :], after) * jnp.where(me + k < n, 1.0, 0.0)
            norm = norm + w * got_hmsg[k - 1, 0:H, :]
        drift_s[...] = norm

    items = [(kind, c) for kind in (0, 1) for c in range(chunks)]
    drain = LAG * last_round
    key_from = chunks + drain + 3
    total = jnp.zeros((F, DH), F32)
    keys_done = 0
    for wave in range(len(items) + drain):
        for r in range(last_round + 1):
            if 0 <= wave - LAG * r < len(items):
                finish(*items[wave - LAG * r], r)
        if wave < chunks:
            if 2 <= wave + 2 < chunks:
                scores(wave + 2)
            adjoint(wave)
        if wave + AHEAD < len(items):
            start(*items[wave + AHEAD], 0)
        if 0 <= wave - drain < chunks:
            total = query_side(wave - drain, total)
        if wave - drain == chunks - 1:
            for copy in drifts:
                copy.start()
        if wave == key_from:
            take_drifts()
        if 0 <= wave - drain - chunks:
            key_first(wave - drain - chunks)
        if wave >= key_from:
            for _ in range(2):
                if keys_done <= wave - drain - chunks:
                    total = key_side(keys_done, total)
                    keys_done += 1
    for c in range(keys_done, chunks):
        total = key_side(c, total)

    half = F // dp
    acc[...] = total
    mine = pl.ds(row * half, half)
    theirs = pl.ds((1 - row) * half, half)
    sums = [pltpu.make_async_remote_copy(
        src_ref=acc.at[theirs], dst_ref=got_half, send_sem=wsend.at[0], recv_sem=wrecv.at[0],
        device_id=other_core, device_id_type=MESH)]
    sums[0].start()
    sums[0].wait_recv()
    total = acc[mine] + got_half[...]
    for r, b in enumerate(hops):
        held[r] = total
        copy = pltpu.make_async_remote_copy(
            src_ref=held.at[r], dst_ref=got_w.at[r], send_sem=wsend.at[r + 1], recv_sem=wrecv.at[r + 1],
            device_id=partner(b), device_id_type=MESH)
        copy.start()
        copy.wait_recv()
        sums.append(copy)
        total = total + got_w[r]
    steps = len(hops)
    held[steps] = total
    copy = pltpu.make_async_remote_copy(
        src_ref=held.at[steps], dst_ref=got_final, send_sem=wsend.at[steps + 1], recv_sem=wrecv.at[steps + 1],
        device_id=other_core, device_id_type=MESH)
    copy.start()
    sums.append(copy)
    copy.wait_recv()
    for copy in sums:
        copy.wait_send()
    acc[mine] = total
    acc[theirs] = got_final[...]
    whole = acc[...]
    scale = lax.rsqrt(jnp.sum(whole * whole, keepdims=True) / (DH * F) + EPSILON)
    new_ref[...] = weight.astype(F32) - RATE * whole * scale

    for copy in small + drifts:
        copy.wait_send()
    for kind, c in items:
        for r in range(last_round):
            copy_of(kind, c, r).wait_send()

        @pl.when(can_up if kind == 0 else can_down)
        def _():
            copy_of(kind, c, last_round).wait_send()


def hand_on(*refs):
    for source, target in zip(refs[:4], refs[4:]):
        target[...] = source[...]


def shards(n, dp, queries, keys, values, doc_ids, feat_weight, out_grad):
    tokens = queries.shape[1]
    wide = H * DH
    group = max(2, n // 4)
    q, k, v, g = (x.reshape(tokens, wide) for x in (queries, keys, values, out_grad))
    rounds = len(bits(group))
    steps = len(bits(n))
    slots = 2 * (H // CHUNK) * (rounds + 1)
    shape = jax.ShapeDtypeStruct
    vmem = pl.BlockSpec(memory_space=pltpu.VMEM)
    dma = pltpu.SemaphoreType.DMA
    results = pl.pallas_call(
        functools.partial(kernel, n, dp, group),
        in_specs=[pl.BlockSpec(memory_space=pltpu.SMEM)] + [vmem] * 5,
        out_specs=[vmem] * 5,
        out_shape=[shape((tokens, wide), F32)] * 4 + [shape((F, DH), F32)],
        scratch_shapes=[
            pltpu.VMEM((H, tokens, F), BF),
            pltpu.VMEM((H, tokens, F), BF),
            pltpu.VMEM((H, tokens, tokens), BF),
            pltpu.VMEM((tokens, wide), F32),
            pltpu.VMEM((H, F, DH), F32),
            pltpu.VMEM((H, F, DH), F32),
            pltpu.VMEM((H, 256), F32),
            pltpu.VMEM((H, tokens, F), F32),
            pltpu.VMEM((H, 256), F32),
            pltpu.VMEM((H + 8, 256), F32),
            pltpu.VMEM((8, 256), F32),
            pltpu.VMEM((2 * group + 1, 8, 256), F32),
            pltpu.VMEM((group, H + 8, 256), F32),
            pltpu.VMEM((group, 8, 256), F32),
            pltpu.VMEM((H + 8, 256), F32),
            pltpu.VMEM((group, H + 8, 256), F32),
            pltpu.VMEM((2, H, F, DH), F32),
            pltpu.VMEM((2, max(1, rounds - 1), H, F, DH), F32),
            pltpu.VMEM((2, H, F, DH), F32),
            pltpu.VMEM((2, rounds + 1, H, F, DH), F32),
            pltpu.VMEM((F, DH), F32),
            pltpu.VMEM((steps + 1, F // dp, DH), F32),
            pltpu.VMEM((steps, F // dp, DH), F32),
            pltpu.VMEM((F // dp, DH), F32),
            pltpu.VMEM((F // dp, DH), F32),
            dma((group,)), dma((group,)), dma((group,)), dma((group,)), dma((group,)), dma((group,)),
            dma((slots,)), dma((slots,)), dma((steps + 2,)), dma((steps + 2,)),
        ],
        compiler_params=pltpu.CompilerParams(
            collective_id=0, has_side_effects=True, vmem_limit_bytes=LIMIT),
    )(doc_ids, q, k, v, g, feat_weight.T)
    cols = pl.BlockSpec((tokens, wide // 4), lambda i: (0, i))
    placed = pl.pallas_call(
        hand_on,
        grid=(4,),
        in_specs=[cols] * 4,
        out_specs=[cols] * 4,
        out_shape=[shape((tokens, wide), F32)] * 4,
        compiler_params=pltpu.CompilerParams(vmem_limit_bytes=LIMIT),
    )(*results[:4])
    full = (1, tokens, wide)
    return tuple(x.reshape(full) for x in placed) + (results[4].T,)


def solution(mesh):
    split = P("dp", "ctx", None)
    return jax.shard_map(
        functools.partial(shards, mesh.shape["ctx"], mesh.shape["dp"]),
        mesh=mesh,
        in_specs=(split, split, split, P("dp", "ctx"), P(), split),
        out_specs=(split, split, split, split, P()),
        check_vma=False,
    )
```

```python
import functools

import jax
import jax.numpy as jnp
from jax import lax
from jax.experimental import pallas as pl
from jax.experimental.pallas import tpu as pltpu
from jax.sharding import PartitionSpec as P

H = 16
DH = 128
F = 160
BLOCK = 64
RATE = 0.5
EPSILON = 1e-06
CHUNK = 2
LAG = 2
AHEAD = 3
MESH = pl.DeviceIdType.MESH
BF = jnp.bfloat16
F32 = jnp.float32
LIMIT = 56 * 1024 * 1024


def dot(a, b, dims):
    return lax.dot_general(a, b, ((dims[:1], dims[1:]), ((), ())), preferred_element_type=F32)


def features(proj):
    return (1.0 + proj + 0.5 * proj * proj).astype(BF)


def row_docs(doc_ref, shape, dim):
    place = lax.broadcasted_iota(jnp.int32, shape, dim) // BLOCK
    docs = jnp.zeros(shape, F32)
    for block in range(doc_ref.shape[1]):
        docs = jnp.where(place == block, doc_ref[0, block].astype(F32), docs)
    return docs


def same(a, b):
    return jnp.where(a == b, 1.0, 0.0)


def bits(count):
    return [1 << r for r in range(count.bit_length() - 1)]


def kernel(
    n, dp, group, doc_ref, q_ref, k_ref, v_ref, g_ref, w_ref,
    out_ref, qg_ref, kg_ref, vg_ref, new_ref,
    fq, fk, slope_q, slope_k, probs_s, scaled_s, den_s, s_s, a_s, nin_s, hn_s, drift_s,
    msg, note, table, got_msg, got_note, hmsg, got_hmsg,
    own_sum, part, suffix, got, acc, held, got_w, got_half, got_final,
    ms, mr, ns, nr, hs, hr, send, recv, wsend, wrecv,
):
    me = lax.axis_index("ctx")
    row = lax.axis_index("dp")
    tokens = q_ref.shape[0]
    rounds = bits(group)
    last_round = len(rounds)
    chunks = H // CHUNK
    hops = bits(n)

    def partner(b):
        return {"ctx": me + b - 2 * b * lax.rem(me // b, 2)}

    other_core = {"dp": 1 - row}

    barrier = pltpu.get_barrier_semaphore()
    greeted = 2 * group + 1
    for k in range(1, group + 1):
        for target in (lax.rem(me + k, n), lax.rem(me + n - k, n)):
            pl.semaphore_signal(barrier, inc=1, device_id={"ctx": target}, device_id_type=MESH)
    pl.semaphore_signal(barrier, inc=1, device_id=other_core, device_id_type=MESH)
    for b in hops:
        if b > group:
            greeted += 1
            pl.semaphore_signal(barrier, inc=1, device_id=partner(b), device_id_type=MESH)

    last = doc_ref[0, doc_ref.shape[1] - 1].astype(F32)
    first = doc_ref[0, 0].astype(F32)
    which = lax.broadcasted_iota(jnp.int32, (8, 256), 0)
    tile = jnp.where(which == 0, last, jnp.where(which == 1, first, 0.0))
    note[...] = tile
    table[group] = tile
    msg[H : H + 8, :] = tile
    hmsg[H : H + 8, :] = tile
    rows = row_docs(doc_ref, (tokens, 1), 0)
    mask = jnp.logical_and(
        lax.broadcasted_iota(jnp.int32, (tokens, tokens), 1)
        <= lax.broadcasted_iota(jnp.int32, (tokens, tokens), 0),
        rows == row_docs(doc_ref, (1, tokens), 1),
    )
    tail = same(rows, last)
    head = same(rows, first)
    weight = w_ref[...]
    ones = jnp.ones((tokens, DH), BF)
    zeros = jnp.zeros((1, 256 - F), F32)

    def heads_of(c):
        return range(c * CHUNK, (c + 1) * CHUNK)

    def columns(h):
        return slice(h * DH, (h + 1) * DH)

    def copy_of(kind, c, r):
        heads = pl.ds(c * CHUNK, CHUNK)
        if r < last_round:
            target = partner(rounds[r])
        else:
            target = {"ctx": me + group if kind == 0 else me - group}
        if r == 0:
            source = own_sum.at[kind, heads]
        elif r < last_round:
            source = part.at[kind, r - 1, heads]
        else:
            source = suffix.at[kind, heads]
        slot = (kind * chunks + c) * (last_round + 1) + r
        return pltpu.make_async_remote_copy(
            src_ref=source, dst_ref=got.at[kind, r, heads], send_sem=send.at[slot], recv_sem=recv.at[slot],
            device_id=target, device_id_type=MESH)

    can_up = me + group < n
    can_down = me >= group

    def start(kind, c, r):
        if r < last_round:
            copy_of(kind, c, r).start()
        else:
            @pl.when(can_up if kind == 0 else can_down)
            def _():
                copy_of(kind, c, r).start()

    for h in range(H):
        proj = dot(k_ref[:, columns(h)], weight, (1, 1))
        slope_k[h] = 1.0 + proj
        feat = features(proj)
        fk[h] = feat
        line = jnp.sum(feat.astype(F32) * tail, axis=0, keepdims=True)
        msg[h : h + 1, :] = jnp.concatenate([line, zeros], axis=1)
    pl.semaphore_wait(barrier, greeted)

    small = []
    for k in range(1, group + 1):
        small.append(pltpu.make_async_remote_copy(
            src_ref=msg, dst_ref=got_msg.at[k - 1], send_sem=ms.at[k - 1], recv_sem=mr.at[k - 1],
            device_id={"ctx": lax.rem(me + k, n)}, device_id_type=MESH))
        small.append(pltpu.make_async_remote_copy(
            src_ref=note, dst_ref=got_note.at[k - 1], send_sem=ns.at[k - 1], recv_sem=nr.at[k - 1],
            device_id={"ctx": lax.rem(me + n - k, n)}, device_id_type=MESH))
    for copy in small:
        copy.start()
    for c in range(chunks):
        for h in heads_of(c):
            tail_k = (fk[h].astype(F32) * tail).astype(BF)
            own_sum[0, h] = dot(tail_k, v_ref[:, columns(h)], (0, 0))
        if c < AHEAD:
            start(0, c, 0)

    def scores(c):
        for h in heads_of(c):
            proj = dot(q_ref[:, columns(h)], weight, (1, 1))
            slope_q[h] = 1.0 + proj
            feat_q = features(proj)
            probs = jnp.where(mask, dot(feat_q, fk[h], (1, 1)), 0.0).astype(BF)
            fq[h] = feat_q
            probs_s[h] = probs
            den_s[:, columns(h)] = dot(probs, ones, (1, 0))

    scores(0)
    scores(1)
    for copy in small:
        copy.wait_recv()
    for k in range(1, group + 1):
        table[group - k] = got_msg[k - 1, H : H + 8, :]
        table[group + k] = got_note[k - 1]

    def doc_at(index, kind):
        return table[index - me + group][kind : kind + 1, :]

    before = table[group - 1][0:1, :]
    after = table[group + 1][1:2, :]
    norm = jnp.zeros((H, 256), F32)
    for k in range(1, group + 1):
        w = same(got_msg[k - 1, H : H + 1, :], before) * jnp.where(me >= k, 1.0, 0.0)
        norm = norm + w * got_msg[k - 1, 0:H, :]
    nin_s[...] = norm
    inside = same(rows, before[:, :DH])
    beyond = same(rows, after[:, :DH])
    inside_f = inside[:, 0:1]
    beyond_f = beyond[:, 0:1]

    def adjoint(c):
        for h in heads_of(c):
            feat = fq[h].astype(F32)
            extra = jnp.sum(feat * nin_s[h : h + 1, :F], axis=1, keepdims=True)
            den = den_s[:, columns(h)] + inside * extra
            den_s[:, columns(h)] = den
            scaled = (g_ref[:, columns(h)].astype(F32) / den).astype(BF)
            scaled_s[h] = scaled
            own_sum[1, h] = dot((feat * head).astype(BF), scaled, (0, 0))

    weights = {}
    for kind in (0, 1):
        near = before if kind == 0 else after
        for r, b in enumerate(rounds):
            u = lax.rem(me // b, 2)
            own = (me // b) * b
            other = own + b - 2 * b * u
            shift = b - 1 if kind == 0 else 0
            far = doc_at(other + shift, kind)
            w = same(doc_at(own + shift, kind), far)[:, :DH]
            wp = same(far, near)[:, :DH]
            up = (u if kind == 0 else 1 - u).astype(F32)
            keep = up + (1.0 - up) * w
            weights[kind, r] = (up * wp, keep, 1.0 - up, up * w + (1.0 - up))
        base = (me // group) * group
        far = doc_at(base - 1 if kind == 0 else base + group, kind)
        weights[kind, last_round] = same(far, near)[:, :DH]

    def finish(kind, c, r):
        heads = pl.ds(c * CHUNK, CHUNK)
        result = s_s if kind == 0 else a_s
        copy = copy_of(kind, c, r)
        if r == last_round:
            @pl.when(can_down if kind == 0 else can_up)
            def _():
                copy.wait_recv()
                result[heads] = result[heads] + weights[kind, r] * got[kind, r, heads]
            return
        copy.wait_recv()
        wp, keep, take, add = weights[kind, r]
        for h in heads_of(c):
            came = got[kind, r, h]
            if r == 0:
                mine = own_sum[kind, h]
                result[h] = wp * came
                suffix[kind, h] = keep * mine + take * came
            else:
                mine = part[kind, r - 1, h]
                result[h] = result[h] + wp * came
                suffix[kind, h] = keep * suffix[kind, h] + take * came
            if r + 1 < last_round:
                part[kind, r, h] = keep * mine + add * came
        start(kind, c, r + 1)

    def query_side(c, total):
        for h in heads_of(c):
            grad = g_ref[:, columns(h)].astype(F32)
            feat_q = fq[h]
            den = den_s[:, columns(h)]
            value = v_ref[:, columns(h)]
            query = q_ref[:, columns(h)]
            state = s_s[h].astype(BF)
            carried = dot(feat_q, state, (1, 0))
            out = (dot(probs_s[h], value, (1, 0)) + inside * carried) / den
            out_ref[:, columns(h)] = out
            drift = -jnp.sum(grad * out, axis=1, keepdims=True) / den[:, 0:1]
            line = jnp.sum(feat_q.astype(F32) * (head * drift), axis=0, keepdims=True)
            hmsg[h : h + 1, :] = jnp.concatenate([line, zeros], axis=1)
            high = scaled_s[h]
            dprobs = jnp.where(mask, dot(high, value, (1, 1)) + drift, 0.0).astype(BF)
            cross = dot(high, state, (1, 1))
            grad_fq = dot(dprobs, fk[h], (1, 0)) + inside_f * (cross + nin_s[h : h + 1, :F] * drift)
            hn_s[h] = dot(dprobs, feat_q, (0, 0))
            vg_ref[:, columns(h)] = dot(probs_s[h], high, (0, 0))
            grad_pq = (grad_fq * slope_q[h]).astype(BF)
            qg_ref[:, columns(h)] = dot(grad_pq, weight, (1, 0))
            total = total + dot(grad_pq, query, (0, 0))
        return total

    def key_first(c):
        for h in heads_of(c):
            value = v_ref[:, columns(h)]
            adj = a_s[h].astype(BF)
            later = dot(fk[h], adj, (1, 0))
            vg_ref[:, columns(h)] = vg_ref[:, columns(h)] + beyond * later
            from_later = dot(value, adj, (1, 1))
            hn_s[h] = hn_s[h] + beyond_f * from_later

    def key_side(c, total):
        for h in heads_of(c):
            key = k_ref[:, columns(h)]
            grad_fk = hn_s[h] + beyond_f * drift_s[h : h + 1, :F]
            grad_pk = (grad_fk * slope_k[h]).astype(BF)
            kg_ref[:, columns(h)] = dot(grad_pk, weight, (1, 0))
            total = total + dot(grad_pk, key, (0, 0))
        return total

    drifts = []
    for k in range(1, group + 1):
        drifts.append(pltpu.make_async_remote_copy(
            src_ref=hmsg, dst_ref=got_hmsg.at[k - 1], send_sem=hs.at[k - 1], recv_sem=hr.at[k - 1],
            device_id={"ctx": lax.rem(me + n - k, n)}, device_id_type=MESH))

    def take_drifts():
        for copy in drifts:
            copy.wait_recv()
        norm = jnp.zeros((H, 256), F32)
        for k in range(1, group + 1):
            w = same(got_hmsg[k - 1, H + 1 : H + 2, :], after) * jnp.where(me + k < n, 1.0, 0.0)
            norm = norm + w * got_hmsg[k - 1, 0:H, :]
        drift_s[...] = norm

    items = [(kind, c) for kind in (0, 1) for c in range(chunks)]
    drain = LAG * last_round
    key_from = chunks + drain + 3
    total = jnp.zeros((F, DH), F32)
    keys_done = 0
    for wave in range(len(items) + drain):
        for r in range(last_round + 1):
            if 0 <= wave - LAG * r < len(items):
                finish(*items[wave - LAG * r], r)
        if wave < chunks:
            if 2 <= wave + 2 < chunks:
                scores(wave + 2)
            adjoint(wave)
        if wave + AHEAD < len(items):
            start(*items[wave + AHEAD], 0)
        if 0 <= wave - drain < chunks:
            total = query_side(wave - drain, total)
        if wave - drain == chunks - 1:
            for copy in drifts:
                copy.start()
        if wave == key_from:
            take_drifts()
        if 0 <= wave - drain - chunks:
            key_first(wave - drain - chunks)
        if wave >= key_from:
            for _ in range(2):
                if keys_done <= wave - drain - chunks:
                    total = key_side(keys_done, total)
                    keys_done += 1
    for c in range(keys_done, chunks):
        total = key_side(c, total)

    half = F // dp
    acc[...] = total
    mine = pl.ds(row * half, half)
    theirs = pl.ds((1 - row) * half, half)
    sums = [pltpu.make_async_remote_copy(
        src_ref=acc.at[theirs], dst_ref=got_half, send_sem=wsend.at[0], recv_sem=wrecv.at[0],
        device_id=other_core, device_id_type=MESH)]
    sums[0].start()
    sums[0].wait_recv()
    total = acc[mine] + got_half[...]
    for r, b in enumerate(hops):
        held[r] = total
        copy = pltpu.make_async_remote_copy(
            src_ref=held.at[r], dst_ref=got_w.at[r], send_sem=wsend.at[r + 1], recv_sem=wrecv.at[r + 1],
            device_id=partner(b), device_id_type=MESH)
        copy.start()
        copy.wait_recv()
        sums.append(copy)
        total = total + got_w[r]
    steps = len(hops)
    held[steps] = total
    copy = pltpu.make_async_remote_copy(
        src_ref=held.at[steps], dst_ref=got_final, send_sem=wsend.at[steps + 1], recv_sem=wrecv.at[steps + 1],
        device_id=other_core, device_id_type=MESH)
    copy.start()
    sums.append(copy)
    copy.wait_recv()
    for copy in sums:
        copy.wait_send()
    acc[mine] = total
    acc[theirs] = got_final[...]
    whole = acc[...]
    scale = lax.rsqrt(jnp.sum(whole * whole, keepdims=True) / (DH * F) + EPSILON)
    new_ref[...] = weight.astype(F32) - RATE * whole * scale

    for copy in small + drifts:
        copy.wait_send()
    for kind, c in items:
        for r in range(last_round):
            copy_of(kind, c, r).wait_send()

        @pl.when(can_up if kind == 0 else can_down)
        def _():
            copy_of(kind, c, last_round).wait_send()


def hand_on(*refs):
    for source, target in zip(refs[:4], refs[4:]):
        target[...] = source[...]


def shards(n, dp, queries, keys, values, doc_ids, feat_weight, out_grad):
    tokens = queries.shape[1]
    wide = H * DH
    group = max(2, n // 4)
    q, k, v, g = (x.reshape(tokens, wide) for x in (queries, keys, values, out_grad))
    rounds = len(bits(group))
    steps = len(bits(n))
    slots = 2 * (H // CHUNK) * (rounds + 1)
    shape = jax.ShapeDtypeStruct
    vmem = pl.BlockSpec(memory_space=pltpu.VMEM)
    dma = pltpu.SemaphoreType.DMA
    results = pl.pallas_call(
        functools.partial(kernel, n, dp, group),
        in_specs=[pl.BlockSpec(memory_space=pltpu.SMEM)] + [vmem] * 5,
        out_specs=[vmem] * 5,
        out_shape=[shape((tokens, wide), F32)] * 4 + [shape((F, DH), F32)],
        scratch_shapes=[
            pltpu.VMEM((H, tokens, F), BF),
            pltpu.VMEM((H, tokens, F), BF),
            pltpu.VMEM((H, tokens, F), F32),
            pltpu.VMEM((H, tokens, F), F32),
            pltpu.VMEM((H, tokens, tokens), BF),
            pltpu.VMEM((H, tokens, DH), BF),
            pltpu.VMEM((tokens, wide), F32),
            pltpu.VMEM((H, F, DH), F32),
            pltpu.VMEM((H, F, DH), F32),
            pltpu.VMEM((H, 256), F32),
            pltpu.VMEM((H, tokens, F), F32),
            pltpu.VMEM((H, 256), F32),
            pltpu.VMEM((H + 8, 256), F32),
            pltpu.VMEM((8, 256), F32),
            pltpu.VMEM((2 * group + 1, 8, 256), F32),
            pltpu.VMEM((group, H + 8, 256), F32),
            pltpu.VMEM((group, 8, 256), F32),
            pltpu.VMEM((H + 8, 256), F32),
            pltpu.VMEM((group, H + 8, 256), F32),
            pltpu.VMEM((2, H, F, DH), F32),
            pltpu.VMEM((2, max(1, rounds - 1), H, F, DH), F32),
            pltpu.VMEM((2, H, F, DH), F32),
            pltpu.VMEM((2, rounds + 1, H, F, DH), F32),
            pltpu.VMEM((F, DH), F32),
            pltpu.VMEM((steps + 1, F // dp, DH), F32),
            pltpu.VMEM((steps, F // dp, DH), F32),
            pltpu.VMEM((F // dp, DH), F32),
            pltpu.VMEM((F // dp, DH), F32),
            dma((group,)), dma((group,)), dma((group,)), dma((group,)), dma((group,)), dma((group,)),
            dma((slots,)), dma((slots,)), dma((steps + 2,)), dma((steps + 2,)),
        ],
        compiler_params=pltpu.CompilerParams(
            collective_id=0, has_side_effects=True, vmem_limit_bytes=LIMIT),
    )(doc_ids, q, k, v, g, feat_weight.T)
    cols = pl.BlockSpec((tokens, wide // 8), lambda i: (0, i))
    placed = pl.pallas_call(
        hand_on,
        grid=(8,),
        in_specs=[cols] * 4,
        out_specs=[cols] * 4,
        out_shape=[shape((tokens, wide), F32)] * 4,
        compiler_params=pltpu.CompilerParams(vmem_limit_bytes=LIMIT),
    )(*results[:4])
    full = (1, tokens, wide)
    return tuple(x.reshape(full) for x in placed) + (results[4].T,)


def solution(mesh):
    split = P("dp", "ctx", None)
    return jax.shard_map(
        functools.partial(shards, mesh.shape["ctx"], mesh.shape["dp"]),
        mesh=mesh,
        in_specs=(split, split, split, P("dp", "ctx"), P(), split),
        out_specs=(split, split, split, split, P()),
        check_vma=False,
    )
```
